32 devices in a mesh: seq: 8 (over y, x, core), head: 4 (over z).
Axes of the slice: x: 2, y: 2, z: 4, core: 2. Of those that a mesh axis runs over, the one named last changes fastest.
Arguments:
- tokens: bfloat16 [16384, 2048], P(('seq', 'head')), may hold values from -6 to 6
- w_query: bfloat16 [2048, 2048], P(None, 'head'), may hold values from -0.125 to 0.125
- w_key: bfloat16 [2048, 2048], P(None, 'head'), may hold values from -0.125 to 0.125
- w_value: bfloat16 [2048, 2048], P(None, 'head'), may hold values from -0.125 to 0.125
- w_beta: bfloat16 [2048, 16], P(None, 'head'), may hold values from -0.125 to 0.125
- beta_gain: float32 [16], P('head'), may hold values from 0.0005 to 0.5
- norm_gain: float32 [2048], P('head'), may hold values from 0.1 to 1.9
- w_out: bfloat16 [2048, 2048], P('head'), may hold values from -0.125 to 0.125
Outputs:
- mixed: bfloat16 [16384, 2048], P(('seq', 'head'))
The draws below stay inside these ranges and needn't reach their ends.
All inputs are finite; a program needn't handle non-finite values.
Results may differ from the reference program's by a relative error of at most 0.0085.
Values may be sent and summed in bfloat16 or wider, within the bound.
A program may use at most 192 MiB of HBM per device.

```python
import math
import jax
import jax.numpy as jnp
from jax import lax

D = 2048
H = 16
DK = 128
SPAN = 64
TOKENS = 16384


def levels(stream_key, shape, pieces, smallest, largest):
    def one(position, blocks):
        draws = jax.random.uniform(jax.random.fold_in(jax.random.fold_in(stream_key, 6), position), (blocks,), jnp.float32, smallest / len(pieces), largest / len(pieces))
        return jnp.repeat(jnp.exp(draws), shape[position] // blocks).reshape((-1,) + (1,) * (len(shape) - position - 1))

    level = one(*pieces[0])
    for cut in pieces[1:]:
        level = level * one(*cut)
    return level


def bell_draw(rng, shape, spread, most, split=(), held_as=jnp.bfloat16):
    gain = levels(rng, shape, split, -0.22, 0.18) if split else 1.0
    result = jax.random.normal(rng, shape, jnp.float32) * spread * gain
    return jnp.minimum(jnp.maximum(result, -most), most).astype(held_as)


def setup_inputs(seed: int = 0) -> dict:
    arg_keys = jax.random.split(jax.random.key(seed), 9)
    tokens = bell_draw(arg_keys[0], (TOKENS, D), 1.0, 6.0, ((0, 32),))
    w_query = bell_draw(arg_keys[1], (D, D), D ** -0.5, 0.125, ((1, 4),))
    w_key = bell_draw(arg_keys[2], (D, D), D ** -0.5, 0.125, ((1, 4),))
    w_value = bell_draw(arg_keys[3], (D, D), D ** -0.5, 0.125, ((1, 4),))
    w_beta = bell_draw(arg_keys[4], (D, H), D ** -0.5, 0.125, ((1, 4),))
    beta_gain = jnp.clip(jnp.exp(math.log(0.5) - 6.9077552 * jax.random.uniform(arg_keys[5], (H,), jnp.float32) ** levels(arg_keys[5], (H,), ((0, 4),), -0.2, 0.2)), 0.0005, 0.5)
    norm_gain = jnp.clip(1.0 + 0.18 * jax.random.normal(arg_keys[6], (D,), jnp.float32), 0.1, 1.9)
    w_out = bell_draw(arg_keys[7], (D, D), D ** -0.5, 0.125, ((0, 4),))
    return {"tokens": tokens, "w_query": w_query, "w_key": w_key, "w_value": w_value, "w_beta": w_beta, "beta_gain": beta_gain, "norm_gain": norm_gain, "w_out": w_out}


highest = lax.Precision.HIGHEST

def mat(left, right):
    return jnp.einsum('...ij,...jk->...ik', left, right, precision=highest)

def mat_t(left, right):
    return jnp.einsum('...ji,...jk->...ik', left, right, precision=highest)

def mat_bt(left, right):
    return jnp.einsum('...ij,...kj->...ik', left, right, precision=highest)

def unit_norm(raw):
    return raw / jnp.sqrt(lax.optimization_barrier(jnp.sum(raw * raw, -1, keepdims=True)) + 1e-06)

def rounded(array):
    stored = array.astype(jnp.bfloat16)
    return lax.optimization_barrier(stored).astype(jnp.float32)

def span_terms(keys, values, rates):
    size = keys.shape[-2]
    eye = jnp.eye(size, dtype=keys.dtype)
    lower = jnp.tril(rates[..., :, None] * mat_bt(keys, keys), -1)
    inverse = eye - lower
    power = lower
    for level in range(size.bit_length() - 2):
        power = mat(power, power)
        inverse = mat(inverse, eye + power)
    weights = mat(inverse, rates[..., :, None] * keys)
    updates = mat(inverse, rates[..., :, None] * values)
    return (weights, updates)

def head_out(blocks):
    query, key, weights, updates = blocks
    size = query.shape[1]
    width = query.shape[2]
    causal = jnp.tril(jnp.ones((size, size), query.dtype))

    def emit(state, inputs):
        q_blk, k_blk, w_blk, u_blk = inputs
        fresh = u_blk - mat(w_blk, state)
        out = mat(q_blk, state) + mat(causal * mat_bt(q_blk, k_blk), fresh)
        return (state + mat_t(k_blk, fresh), out)
    start = jnp.zeros((width, width), query.dtype)
    final, outs = lax.scan(emit, start, (query, key, weights, updates))
    return outs

def reference(tokens, w_query, w_key, w_value, w_beta, beta_gain, norm_gain, w_out):
    total = tokens.shape[0]

    def project(weight):
        stored = jnp.dot(tokens, weight, preferred_element_type=jnp.float32).astype(jnp.bfloat16)
        return lax.optimization_barrier(stored).astype(jnp.float32).reshape(total, H, DK)
    query = rounded(unit_norm(project(w_query)))
    key = rounded(unit_norm(project(w_key)))
    value = project(w_value)
    beta = beta_gain[None, :] * jax.nn.sigmoid(jnp.dot(tokens, w_beta, preferred_element_type=jnp.float32))
    count = total // SPAN

    def blocks(array):
        return array.reshape(count, SPAN, H, DK).transpose(2, 0, 1, 3)
    q_blocks = blocks(query)
    k_blocks = blocks(key)
    v_blocks = blocks(value)
    b_blocks = beta.reshape(count, SPAN, H).transpose(2, 0, 1)
    weights, updates = span_terms(k_blocks, v_blocks, b_blocks)
    outs = lax.map(head_out, (q_blocks, k_blocks, weights, updates))
    heads_out = outs.transpose(1, 2, 0, 3).reshape(total, H, DK)
    scaled = heads_out / jnp.sqrt(lax.optimization_barrier(jnp.mean(heads_out * heads_out, -1, keepdims=True)) + 1e-05)
    normed = (scaled * norm_gain.reshape(H, DK)).reshape(total, H * DK).astype(jnp.bfloat16)
    return jnp.dot(normed, w_out, preferred_element_type=jnp.float32).astype(jnp.bfloat16)
```

```python
import functools

import jax
import jax.numpy as jnp
from jax import lax
from jax.experimental import pallas as pl
from jax.experimental.pallas import tpu as pltpu
from jax.sharding import PartitionSpec as P

CHUNK = 256
LANES = 128
VMEM = 48 * 2**20
half = jnp.bfloat16
single = jnp.float32


def mm(left, right):
    return jnp.dot(left.astype(half), right.astype(half), preferred_element_type=single)


def mm_bt(left, right):
    return lax.dot_general(left, right, (((1,), (1,)), ((), ())), preferred_element_type=single)


def mm_t(left, right):
    return lax.dot_general(
        left, right.astype(half), (((0,), (0,)), ((), ())), preferred_element_type=single
    )


def unit(raw):
    return (raw * lax.rsqrt(jnp.sum(raw * raw, -1, keepdims=True) + 1e-06)).astype(half)


def chunk_kernel(heads, tok, wq, wk, wv, wb, gain, reads_ref, outs_ref, trans_ref):
    width = wq.shape[1] // heads
    x = tok[0]
    each = range(heads)

    def project(w):
        full = jnp.dot(x, w[...], preferred_element_type=single).astype(half).astype(single)
        return [full[:, h * width : (h + 1) * width] for h in each]

    k = [unit(a) for a in project(wk)]
    beta = gain[...] * jax.nn.sigmoid(jnp.dot(x, wb[...], preferred_element_type=single))
    rates = [beta[:, h : h + 1] for h in each]
    row = lax.broadcasted_iota(jnp.int32, (CHUNK, CHUNK), 0)
    col = lax.broadcasted_iota(jnp.int32, (CHUNK, CHUNK), 1)
    near = (row // 16) == (col // 16)
    mid = (row // 64) == (col // 64)
    below = row > col
    eye = jnp.where(row == col, 1.0, 0.0).astype(single)
    lower = [jnp.where(below, rates[h] * mm_bt(k[h], k[h]), 0.0) for h in each]
    power = [jnp.where(near, a, 0.0) for a in lower]
    inverse = [eye - a for a in power]
    for level in range(3):
        power = [mm(a, a) for a in power]
        inverse = [t + mm(t, a) for t, a in zip(inverse, power)]
    rest = [mm(t, jnp.where(mid & ~near, a, 0.0)) for t, a in zip(inverse, lower)]
    inverse = [t - mm(r, t) for r, t in zip(rest, inverse)]
    rest = [mm(r, r) for r in rest]
    inverse = [t + mm(r, t) for r, t in zip(rest, inverse)]
    rest = [mm(t, jnp.where(mid, 0.0, a)) for t, a in zip(inverse, lower)]
    v = project(wv)
    terms = [jnp.concatenate([rates[h] * k[h].astype(single), rates[h] * v[h]], 1) for h in each]
    terms = [mm(t, a) for t, a in zip(inverse, terms)]
    terms = [t - mm(r, t) for r, t in zip(rest, terms)]
    rest = [mm(r, r) for r in rest]
    terms = [(t + mm(r, t)).astype(half) for r, t in zip(rest, terms)]
    q = [unit(a) for a in project(wq)]
    for h in each:
        causal = jnp.where(below | (row == col), mm_bt(q[h], k[h]), 0.0)
        read = mm(causal, terms[h])
        here = slice(h * width, (h + 1) * width)
        reads_ref[0, :, here] = (q[h].astype(single) - read[:, :width]).astype(half)
        outs_ref[0, :, here] = read[:, width:]
        trans_ref[0, h] = mm_t(k[h], terms[h])


def chunk_terms(tokens, wq, wk, wv, wb, gain, heads):
    chunks, _, depth = tokens.shape
    per = wq.shape[1]
    width = per // heads

    def once(shape):
        return pl.BlockSpec(shape, lambda i: (0,) * len(shape), pipeline_mode=pl.Buffered(1))

    return pl.pallas_call(
        functools.partial(chunk_kernel, heads),
        grid=(chunks,),
        in_specs=[pl.BlockSpec((1, CHUNK, depth), lambda i: (i, 0, 0))]
        + [once(w.shape) for w in (wq, wk, wv, wb, gain)],
        out_specs=[
            pl.BlockSpec((1, CHUNK, per), lambda i: (i, 0, 0)),
            pl.BlockSpec((1, CHUNK, per), lambda i: (i, 0, 0)),
            pl.BlockSpec((1, heads, width, 2 * width), lambda i: (i, 0, 0, 0)),
        ],
        out_shape=[
            jax.ShapeDtypeStruct((chunks, CHUNK, per), half),
            jax.ShapeDtypeStruct((chunks, CHUNK, per), single),
            jax.ShapeDtypeStruct((chunks, heads, width, 2 * width), single),
        ],
        compiler_params=pltpu.CompilerParams(vmem_limit_bytes=VMEM),
        cost_estimate=pl.CostEstimate(
            flops=2 * chunks * CHUNK * (depth * 3 * per + heads * 18 * CHUNK * CHUNK),
            bytes_accessed=2 * depth * 3 * per + chunks * CHUNK * (2 * depth + 8 * per),
            transcendentals=0,
        ),
        name="chunk_terms",
    )(tokens, wq, wk, wv, wb, gain)


def fold_kernel(parts, *refs):
    trans, (starts_ref, last_ref) = refs[:parts], refs[parts:]
    chunks, heads, width, _ = trans[0].shape
    row = lax.broadcasted_iota(jnp.int32, (width, 2 * width), 0)
    col = lax.broadcasted_iota(jnp.int32, (width, 2 * width), 1)
    state = [jnp.where(row == col, 1.0, 0.0).astype(single) for _ in range(heads)]
    for place in range(chunks):
        for part in range(parts):
            for h in range(heads):
                starts_ref[place, part, h] = state[h]
                step = trans[part][place, h]
                moved = state[h] - mm(step[:, :width], state[h])
                state[h] = moved + jnp.where(col < width, 0.0, step)
    for h in range(heads):
        last_ref[h] = state[h].astype(half)


def fold(trans):
    chunks, heads, width, wide = trans[0].shape
    parts = len(trans)
    return pl.pallas_call(
        functools.partial(fold_kernel, parts),
        out_shape=[
            jax.ShapeDtypeStruct((chunks, parts, heads, width, wide), single),
            jax.ShapeDtypeStruct((heads, width, wide), half),
        ],
        compiler_params=pltpu.CompilerParams(vmem_limit_bytes=VMEM),
        name="fold",
    )(*trans)


def emit_kernel(parts, place_ref, all_ref, starts_ref, gain, *refs):
    reads, outs, results, entry = (
        refs[:parts],
        refs[parts : 2 * parts],
        refs[2 * parts : 3 * parts],
        refs[3 * parts],
    )
    heads, width, _ = entry.shape

    @pl.when(pl.program_id(0) == 0)
    def _():
        entry[...] = jnp.zeros_like(entry)

        def one(turn, carry):
            for h in range(heads):
                pair = all_ref[turn, h]
                entry[h] = mm(pair[:, :width], entry[h]) + pair[:, width:].astype(single)
            return carry

        lax.fori_loop(0, place_ref[0], one, 0)

    for part in range(parts):
        for h in range(heads):
            here = slice(h * width, (h + 1) * width)
            pair = starts_ref[0, part, h]
            state = mm(pair[:, :width], entry[h]) + pair[:, width:]
            o = mm(reads[part][0, :, here], state) + outs[part][0, :, here]
            scale = lax.rsqrt(jnp.mean(o * o, -1, keepdims=True) + 1e-05)
            results[part][0, :, here] = (o * scale * gain[:, here]).astype(half)


def emit(place, everyone, starts, gain, reads, outs):
    parts = len(reads)
    chunks, _, per = reads[0].shape
    _, _, heads, width, wide = starts.shape
    rows = pl.BlockSpec((1, CHUNK, per), lambda i: (i, 0, 0))
    return pl.pallas_call(
        functools.partial(emit_kernel, parts),
        grid=(chunks,),
        in_specs=[
            pl.BlockSpec(memory_space=pltpu.SMEM),
            pl.BlockSpec(
                everyone.shape, lambda i: (0, 0, 0, 0), pipeline_mode=pl.Buffered(1)
            ),
            pl.BlockSpec((1, parts, heads, width, wide), lambda i: (i, 0, 0, 0, 0)),
            pl.BlockSpec((1, per), lambda i: (0, 0)),
        ]
        + [rows] * (2 * parts),
        out_specs=[rows] * parts,
        out_shape=[jax.ShapeDtypeStruct((chunks, CHUNK, per), half)] * parts,
        scratch_shapes=[pltpu.VMEM((heads, width, width), single)],
        compiler_params=pltpu.CompilerParams(vmem_limit_bytes=VMEM),
        name="emit",
    )(place, everyone, starts, gain, *reads, *outs)


def body(seqs, tokens, w_query, w_key, w_value, w_beta, beta_gain, norm_gain, w_out):
    per = w_query.shape[1]
    heads = w_beta.shape[1]
    place = lax.axis_index("seq")
    parts = tokens.shape[0] // CHUNK
    wb = jnp.pad(w_beta, ((0, 0), (0, LANES - heads)))
    gain = jnp.pad(beta_gain, (0, LANES - heads)).reshape(1, LANES)
    pieces = [
        lax.all_gather(tokens[part * CHUNK : (part + 1) * CHUNK], "head", axis=0)
        for part in range(parts)
    ]
    share = per // seqs
    mine = lax.dynamic_slice_in_dim(w_out, place * share, share, 0)
    mine, pieces[-1] = lax.optimization_barrier((mine, pieces[-1]))
    w_whole = lax.all_gather(mine, ("head", "seq"), axis=0, tiled=True)
    done = [chunk_terms(a, w_query, w_key, w_value, wb, gain, heads) for a in pieces]
    starts, last = fold([a[2] for a in done])
    everyone = lax.all_gather(last, "seq", axis=0)
    normed = emit(
        place.reshape(1).astype(jnp.int32),
        everyone,
        starts,
        norm_gain.reshape(1, per),
        [a[0] for a in done],
        [a[1] for a in done],
    )
    mixed = []
    for a in normed:
        rows = lax.all_to_all(a, "head", split_axis=0, concat_axis=2, tiled=True)
        rows = rows.reshape(CHUNK, -1)
        mixed.append(jnp.dot(rows, w_whole, preferred_element_type=single).astype(half))
    return jnp.concatenate(mixed, 0)


def solution(mesh):
    placed = (
        P(("seq", "head"), None),
        P(None, "head"),
        P(None, "head"),
        P(None, "head"),
        P(None, "head"),
        P("head"),
        P("head"),
        P("head", None),
    )
    return jax.shard_map(
        functools.partial(body, mesh.shape["seq"]),
        mesh=mesh,
        in_specs=placed,
        out_specs=P(("seq", "head"), None),
        check_vma=False,
    )
```

```python
import functools

import jax
import jax.numpy as jnp
from jax import lax
from jax.experimental import pallas as pl
from jax.experimental.pallas import tpu as pltpu
from jax.sharding import PartitionSpec as P

CHUNK = 256
LANES = 128
VMEM = 48 * 2**20
half = jnp.bfloat16
single = jnp.float32


def mm(left, right):
    return jnp.dot(left.astype(half), right.astype(half), preferred_element_type=single)


def mm_bt(left, right):
    return lax.dot_general(left, right, (((1,), (1,)), ((), ())), preferred_element_type=single)


def mm_t(left, right):
    return lax.dot_general(
        left, right.astype(half), (((0,), (0,)), ((), ())), preferred_element_type=single
    )


def unit(raw):
    return (raw * lax.rsqrt(jnp.sum(raw * raw, -1, keepdims=True) + 1e-06)).astype(half)


def chunk_kernel(heads, tok, wq, wk, wv, wb, gain, reads_ref, outs_ref, trans_ref):
    width = wq.shape[1] // heads
    x = tok[0]
    each = range(heads)

    def project(w):
        full = jnp.dot(x, w[...], preferred_element_type=single).astype(half).astype(single)
        return [full[:, h * width : (h + 1) * width] for h in each]

    k = [unit(a) for a in project(wk)]
    beta = gain[...] * jax.nn.sigmoid(jnp.dot(x, wb[...], preferred_element_type=single))
    rates = [beta[:, h : h + 1] for h in each]
    row = lax.broadcasted_iota(jnp.int32, (CHUNK, CHUNK), 0)
    col = lax.broadcasted_iota(jnp.int32, (CHUNK, CHUNK), 1)
    near = (row // 16) == (col // 16)
    mid = (row // 64) == (col // 64)
    below = row > col
    eye = jnp.where(row == col, 1.0, 0.0).astype(single)
    lower = [jnp.where(below, rates[h] * mm_bt(k[h], k[h]), 0.0) for h in each]
    power = [jnp.where(near, a, 0.0) for a in lower]
    inverse = [eye - a for a in power]
    for level in range(3):
        power = [mm(a, a) for a in power]
        inverse = [t + mm(t, a) for t, a in zip(inverse, power)]
    rest = [mm(t, jnp.where(mid & ~near, a, 0.0)) for t, a in zip(inverse, lower)]
    inverse = [t - mm(r, t) for r, t in zip(rest, inverse)]
    rest = [mm(r, r) for r in rest]
    inverse = [t + mm(r, t) for r, t in zip(rest, inverse)]
    rest = [mm(t, jnp.where(mid, 0.0, a)) for t, a in zip(inverse, lower)]
    v = project(wv)
    terms = [jnp.concatenate([rates[h] * k[h].astype(single), rates[h] * v[h]], 1) for h in each]
    terms = [mm(t, a) for t, a in zip(inverse, terms)]
    terms = [t - mm(r, t) for r, t in zip(rest, terms)]
    rest = [mm(r, r) for r in rest]
    terms = [(t + mm(r, t)).astype(half) for r, t in zip(rest, terms)]
    q = [unit(a) for a in project(wq)]
    for h in each:
        causal = jnp.where(below | (row == col), mm_bt(q[h], k[h]), 0.0)
        read = mm(causal, terms[h])
        here = slice(h * width, (h + 1) * width)
        reads_ref[0, :, here] = (q[h].astype(single) - read[:, :width]).astype(half)
        outs_ref[0, :, here] = read[:, width:]
        trans_ref[0, h] = mm_t(k[h], terms[h])


def chunk_terms(tokens, wq, wk, wv, wb, gain, heads, group):
    chunks, _, depth = tokens.shape
    width = wq.shape[1] // wb.shape[1]
    per = heads * width
    gain = jnp.pad(gain[group * heads : (group + 1) * heads], (0, LANES - heads))
    gain = gain.reshape(1, LANES)
    wb = wb[:, group * heads : (group + 1) * heads]
    wb = jnp.pad(wb, ((0, 0), (0, LANES - heads)))

    def once(shape):
        return pl.BlockSpec(shape, lambda i: (0,) * len(shape), pipeline_mode=pl.Buffered(1))

    return pl.pallas_call(
        functools.partial(chunk_kernel, heads),
        grid=(chunks,),
        in_specs=[pl.BlockSpec((1, CHUNK, depth), lambda i: (i, 0, 0))]
        + [
            pl.BlockSpec((depth, per), lambda i: (0, group), pipeline_mode=pl.Buffered(1))
            for _ in range(3)
        ]
        + [once(w.shape) for w in (wb, gain)],
        out_specs=[
            pl.BlockSpec((1, CHUNK, per), lambda i: (i, 0, 0)),
            pl.BlockSpec((1, CHUNK, per), lambda i: (i, 0, 0)),
            pl.BlockSpec((1, heads, width, 2 * width), lambda i: (i, 0, 0, 0)),
        ],
        out_shape=[
            jax.ShapeDtypeStruct((chunks, CHUNK, per), half),
            jax.ShapeDtypeStruct((chunks, CHUNK, per), single),
            jax.ShapeDtypeStruct((chunks, heads, width, 2 * width), single),
        ],
        compiler_params=pltpu.CompilerParams(vmem_limit_bytes=VMEM),
        cost_estimate=pl.CostEstimate(
            flops=2 * chunks * CHUNK * (depth * 3 * per + heads * 18 * CHUNK * CHUNK),
            bytes_accessed=2 * depth * 3 * per + chunks * CHUNK * (2 * depth + 8 * per),
            transcendentals=0,
        ),
        name="chunk_terms",
    )(tokens, wq, wk, wv, wb, gain)


def fold_kernel(parts, *refs):
    trans, (starts_ref, last_ref) = refs[:parts], refs[parts:]
    chunks, heads, width, _ = trans[0].shape
    row = lax.broadcasted_iota(jnp.int32, (width, 2 * width), 0)
    col = lax.broadcasted_iota(jnp.int32, (width, 2 * width), 1)
    state = [jnp.where(row == col, 1.0, 0.0).astype(single) for _ in range(heads)]
    for place in range(chunks):
        for part in range(parts):
            for h in range(heads):
                starts_ref[place, part, h] = state[h]
                step = trans[part][place, h]
                moved = state[h] - mm(step[:, :width], state[h])
                state[h] = moved + jnp.where(col < width, 0.0, step)
    for h in range(heads):
        last_ref[h] = state[h].astype(half)


def fold(trans):
    chunks, heads, width, wide = trans[0].shape
    parts = len(trans)
    return pl.pallas_call(
        functools.partial(fold_kernel, parts),
        out_shape=[
            jax.ShapeDtypeStruct((chunks, parts, heads, width, wide), single),
            jax.ShapeDtypeStruct((heads, width, wide), half),
        ],
        compiler_params=pltpu.CompilerParams(vmem_limit_bytes=VMEM),
        name="fold",
    )(*trans)


def emit_kernel(parts, place_ref, all_ref, starts_ref, gain, *refs):
    reads, outs, (result, entry) = refs[:parts], refs[parts : 2 * parts], refs[2 * parts :]
    heads, width, _ = entry.shape

    @pl.when(pl.program_id(0) == 0)
    def _():
        entry[...] = jnp.zeros_like(entry)

        def one(turn, carry):
            for h in range(heads):
                pair = all_ref[turn, h]
                entry[h] = mm(pair[:, :width], entry[h]) + pair[:, width:].astype(single)
            return carry

        lax.fori_loop(0, place_ref[0], one, 0)

    for part in range(parts):
        for h in range(heads):
            here = slice(h * width, (h + 1) * width)
            pair = starts_ref[0, part, h]
            state = mm(pair[:, :width], entry[h]) + pair[:, width:]
            o = mm(reads[part][0, :, here], state) + outs[part][0, :, here]
            scale = lax.rsqrt(jnp.mean(o * o, -1, keepdims=True) + 1e-05)
            rows = slice(part * CHUNK, (part + 1) * CHUNK)
            result[0, rows, here] = (o * scale * gain[:, here]).astype(half)


def emit(place, everyone, starts, gain, reads, outs):
    parts = len(reads)
    chunks, _, per = reads[0].shape
    _, _, heads, width, wide = starts.shape
    rows = pl.BlockSpec((1, CHUNK, per), lambda i: (i, 0, 0))
    return pl.pallas_call(
        functools.partial(emit_kernel, parts),
        grid=(chunks,),
        in_specs=[
            pl.BlockSpec(memory_space=pltpu.SMEM),
            pl.BlockSpec(
                everyone.shape, lambda i: (0, 0, 0, 0), pipeline_mode=pl.Buffered(1)
            ),
            pl.BlockSpec((1, parts, heads, width, wide), lambda i: (i, 0, 0, 0, 0)),
            pl.BlockSpec((1, per), lambda i: (0, 0)),
        ]
        + [rows] * (2 * parts),
        out_specs=pl.BlockSpec((1, parts * CHUNK, per), lambda i: (i, 0, 0)),
        out_shape=jax.ShapeDtypeStruct((chunks, parts * CHUNK, per), half),
        scratch_shapes=[pltpu.VMEM((heads, width, width), single)],
        compiler_params=pltpu.CompilerParams(vmem_limit_bytes=VMEM),
        name="emit",
    )(place, everyone, starts, gain, *reads, *outs)


def mix_kernel(groups, *refs):
    rows, (w, out) = refs[:groups], refs[groups:]
    owners, _, width = rows[0].shape
    total = 0.0
    for owner in range(owners):
        for g in range(groups):
            first = (owner * groups + g) * width
            total += mm(rows[g][owner], w[first : first + width, :])
    out[...] = total.astype(half)


def mix(rows, w_whole):
    depth, columns = w_whole.shape
    count = rows[0].shape[1]
    tile = 512
    return pl.pallas_call(
        functools.partial(mix_kernel, len(rows)),
        grid=(columns // tile,),
        in_specs=[pl.BlockSpec(a.shape, lambda i: (0, 0, 0)) for a in rows]
        + [pl.BlockSpec((depth, tile), lambda i: (0, i))],
        out_specs=pl.BlockSpec((count, tile), lambda i: (0, i)),
        out_shape=jax.ShapeDtypeStruct((count, columns), half),
        compiler_params=pltpu.CompilerParams(vmem_limit_bytes=VMEM),
        name="mix",
    )(*rows, w_whole)


def whole_weight(w_out, seqs, owners):
    per, columns = w_out.shape
    place = lax.axis_index("seq")
    share = per // seqs
    mine = lax.dynamic_slice_in_dim(w_out, place * share, share, 0)
    turned = [mine]
    for shift in range(1, owners):
        pairs = [(i, (i + shift) % owners) for i in range(owners)]
        turned.append(lax.ppermute(mine, "head", pairs))
    turned = jnp.stack(turned)
    owner = lax.axis_index("head")
    held = jnp.stack(
        [
            lax.dynamic_index_in_dim(turned, (owner - i + owners) % owners, 0, False)
            for i in range(owners)
        ]
    )
    levels = seqs.bit_length() - 1
    turns = list(range(1, levels)) + [0]
    for bit in turns:
        pairs = [(i, i ^ (1 << bit)) for i in range(seqs)]
        other = lax.ppermute(held, "seq", pairs)
        upper = (place >> bit) & 1 == 1
        held = jnp.stack([jnp.where(upper, other, held), jnp.where(upper, held, other)])
    axes = [turns[::-1].index(bit) for bit in reversed(range(levels))]
    held = held.transpose([levels] + axes + [levels + 1, levels + 2])
    return held.reshape(owners * per, columns)


def body(seqs, owners, tokens, w_query, w_key, w_value, w_beta, beta_gain, norm_gain, w_out):
    per = w_query.shape[1]
    heads = w_beta.shape[1]
    place = lax.axis_index("seq")
    parts = tokens.shape[0] // CHUNK
    groups = 2
    few = heads // groups
    w_whole = whole_weight(w_out, seqs, owners)
    pieces = [
        lax.all_gather(tokens[part * CHUNK : (part + 1) * CHUNK], "head", axis=0)
        for part in range(parts)
    ]
    weights = (w_query, w_key, w_value, w_beta, beta_gain)
    done = []
    for a in pieces:
        if done:
            a, done[-1] = lax.optimization_barrier((a, done[-1]))
        done.append([chunk_terms(a, *weights, few, g) for g in range(groups)])
    pairs = [fold([a[g][2] for a in done]) for g in range(groups)]
    everyone = [lax.all_gather(last, "seq", axis=0) for _, last in pairs]
    rows = []
    for g in range(groups):
        normed = emit(
            place.reshape(1).astype(jnp.int32),
            everyone[g],
            pairs[g][0],
            norm_gain[g * per // groups : (g + 1) * per // groups].reshape(1, -1),
            [a[g][0] for a in done],
            [a[g][1] for a in done],
        )
        rows.append(lax.all_to_all(normed, "head", split_axis=0, concat_axis=0, tiled=True))
    return mix(rows, w_whole)


def solution(mesh):
    placed = (
        P(("seq", "head"), None),
        P(None, "head"),
        P(None, "head"),
        P(None, "head"),
        P(None, "head"),
        P("head"),
        P("head"),
        P("head", None),
    )
    return jax.shard_map(
        functools.partial(body, mesh.shape["seq"], mesh.shape["head"]),
        mesh=mesh,
        in_specs=placed,
        out_specs=P(("seq", "head"), None),
        check_vma=False,
    )
```

```python
import functools

import jax
import jax.numpy as jnp
from jax import lax
from jax.experimental import pallas as pl
from jax.experimental.pallas import tpu as pltpu
from jax.sharding import PartitionSpec as P

LANES = 128
CHUNKS = (256, 128, 128)
VMEM = 48 * 2**20
half = jnp.bfloat16
single = jnp.float32


def mm(left, right):
    return jnp.dot(left.astype(half), right.astype(half), preferred_element_type=single)


def mm_bt(left, right):
    return lax.dot_general(left, right, (((1,), (1,)), ((), ())), preferred_element_type=single)


def mm_t(left, right):
    return lax.dot_general(
        left, right.astype(half), (((0,), (0,)), ((), ())), preferred_element_type=single
    )


def unit(raw):
    return (raw * lax.rsqrt(jnp.sum(raw * raw, -1, keepdims=True) + 1e-06)).astype(half)


def chunk_kernel(heads, tok, wq, wk, wv, wb, gain, reads_ref, outs_ref, trans_ref):
    width = wq.shape[1] // heads
    x = tok[0]
    size = x.shape[0]
    each = range(heads)

    def project(w):
        full = jnp.dot(x, w[...], preferred_element_type=single).astype(half).astype(single)
        return [full[:, h * width : (h + 1) * width] for h in each]

    k = [unit(a) for a in project(wk)]
    beta = gain[...] * jax.nn.sigmoid(jnp.dot(x, wb[...], preferred_element_type=single))
    rates = [beta[:, h : h + 1] for h in each]
    row = lax.broadcasted_iota(jnp.int32, (size, size), 0)
    col = lax.broadcasted_iota(jnp.int32, (size, size), 1)
    near = (row // 16) == (col // 16)
    mid = (row // 64) == (col // 64)
    below = row > col
    eye = jnp.where(row == col, 1.0, 0.0).astype(single)
    lower = [jnp.where(below, rates[h] * mm_bt(k[h], k[h]), 0.0) for h in each]
    power = [jnp.where(near, a, 0.0) for a in lower]
    inverse = [eye - a for a in power]
    for level in range(3):
        power = [mm(a, a) for a in power]
        inverse = [t + mm(t, a) for t, a in zip(inverse, power)]
    rest = [mm(t, jnp.where(mid & ~near, a, 0.0)) for t, a in zip(inverse, lower)]
    inverse = [t - mm(r, t) for r, t in zip(rest, inverse)]
    rest = [mm(r, r) for r in rest]
    inverse = [t + mm(r, t) for r, t in zip(rest, inverse)]
    rest = [mm(t, jnp.where(mid, 0.0, a)) for t, a in zip(inverse, lower)]
    v = project(wv)
    terms = [jnp.concatenate([rates[h] * k[h].astype(single), rates[h] * v[h]], 1) for h in each]
    terms = [mm(t, a) for t, a in zip(inverse, terms)]
    terms = [t - mm(r, t) for r, t in zip(rest, terms)]
    rest = [mm(r, r) for r in rest]
    terms = [(t + mm(r, t)).astype(half) for r, t in zip(rest, terms)]
    q = [unit(a) for a in project(wq)]
    for h in each:
        causal = jnp.where(below | (row == col), mm_bt(q[h], k[h]), 0.0)
        read = mm(causal, terms[h])
        here = slice(h * width, (h + 1) * width)
        reads_ref[0, :, here] = (q[h].astype(single) - read[:, :width]).astype(half)
        outs_ref[0, :, here] = read[:, width:]
        trans_ref[0, h] = mm_t(k[h], terms[h])


def chunk_terms(tokens, wq, wk, wv, wb, gain, heads, group):
    chunks, size, depth = tokens.shape
    width = wq.shape[1] // wb.shape[1]
    per = heads * width
    gain = jnp.pad(gain[group * heads : (group + 1) * heads], (0, LANES - heads))
    gain = gain.reshape(1, LANES)
    wb = wb[:, group * heads : (group + 1) * heads]
    wb = jnp.pad(wb, ((0, 0), (0, LANES - heads)))

    def once(shape):
        return pl.BlockSpec(shape, lambda i: (0,) * len(shape), pipeline_mode=pl.Buffered(1))

    return pl.pallas_call(
        functools.partial(chunk_kernel, heads),
        grid=(chunks,),
        in_specs=[pl.BlockSpec((1, size, depth), lambda i: (i, 0, 0))]
        + [
            pl.BlockSpec((depth, per), lambda i: (0, group), pipeline_mode=pl.Buffered(1))
            for _ in range(3)
        ]
        + [once(w.shape) for w in (wb, gain)],
        out_specs=[
            pl.BlockSpec((1, size, per), lambda i: (i, 0, 0)),
            pl.BlockSpec((1, size, per), lambda i: (i, 0, 0)),
            pl.BlockSpec((1, heads, width, 2 * width), lambda i: (i, 0, 0, 0)),
        ],
        out_shape=[
            jax.ShapeDtypeStruct((chunks, size, per), half),
            jax.ShapeDtypeStruct((chunks, size, per), single),
            jax.ShapeDtypeStruct((chunks, heads, width, 2 * width), single),
        ],
        compiler_params=pltpu.CompilerParams(vmem_limit_bytes=VMEM),
        cost_estimate=pl.CostEstimate(
            flops=2 * chunks * size * (depth * 3 * per + heads * 18 * size * size),
            bytes_accessed=2 * depth * 3 * per + chunks * size * (2 * depth + 8 * per),
            transcendentals=0,
        ),
        name="chunk_terms",
    )(tokens, wq, wk, wv, wb, gain)


def fold_kernel(parts, *refs):
    trans, (starts_ref, last_ref) = refs[:parts], refs[parts:]
    chunks, heads, width, _ = trans[0].shape
    row = lax.broadcasted_iota(jnp.int32, (width, 2 * width), 0)
    col = lax.broadcasted_iota(jnp.int32, (width, 2 * width), 1)
    state = [jnp.where(row == col, 1.0, 0.0).astype(single) for _ in range(heads)]
    for place in range(chunks):
        for part in range(parts):
            for h in range(heads):
                starts_ref[place, part, h] = state[h]
                step = trans[part][place, h]
                moved = state[h] - mm(step[:, :width], state[h])
                state[h] = moved + jnp.where(col < width, 0.0, step)
    for h in range(heads):
        last_ref[h] = state[h].astype(half)


def fold(trans):
    chunks, heads, width, wide = trans[0].shape
    parts = len(trans)
    return pl.pallas_call(
        functools.partial(fold_kernel, parts),
        out_shape=[
            jax.ShapeDtypeStruct((chunks, parts, heads, width, wide), single),
            jax.ShapeDtypeStruct((heads, width, wide), half),
        ],
        compiler_params=pltpu.CompilerParams(vmem_limit_bytes=VMEM),
        name="fold",
    )(*trans)


def emit_kernel(parts, place_ref, all_ref, starts_ref, gain, *refs):
    reads, outs, (result, entry) = refs[:parts], refs[parts : 2 * parts], refs[2 * parts :]
    heads, width, _ = entry.shape

    @pl.when(pl.program_id(0) == 0)
    def _():
        entry[...] = jnp.zeros_like(entry)

        def one(turn, carry):
            for h in range(heads):
                pair = all_ref[turn, h]
                entry[h] = mm(pair[:, :width], entry[h]) + pair[:, width:].astype(single)
            return carry

        lax.fori_loop(0, place_ref[0], one, 0)

    first = 0
    for part in range(parts):
        rows = slice(first, first + reads[part].shape[1])
        first = rows.stop
        for h in range(heads):
            here = slice(h * width, (h + 1) * width)
            pair = starts_ref[0, part, h]
            state = mm(pair[:, :width], entry[h]) + pair[:, width:]
            o = mm(reads[part][0, :, here], state) + outs[part][0, :, here]
            scale = lax.rsqrt(jnp.mean(o * o, -1, keepdims=True) + 1e-05)
            result[0, rows, here] = (o * scale * gain[:, here]).astype(half)


def emit(place, everyone, starts, gain, reads, outs):
    parts = len(reads)
    chunks, _, per = reads[0].shape
    _, _, heads, width, wide = starts.shape
    rows = [pl.BlockSpec((1, a.shape[1], per), lambda i: (i, 0, 0)) for a in reads]
    count = sum(a.shape[1] for a in reads)
    return pl.pallas_call(
        functools.partial(emit_kernel, parts),
        grid=(chunks,),
        in_specs=[
            pl.BlockSpec(memory_space=pltpu.SMEM),
            pl.BlockSpec(
                everyone.shape, lambda i: (0, 0, 0, 0), pipeline_mode=pl.Buffered(1)
            ),
            pl.BlockSpec((1, parts, heads, width, wide), lambda i: (i, 0, 0, 0, 0)),
            pl.BlockSpec((1, per), lambda i: (0, 0)),
        ]
        + rows * 2,
        out_specs=pl.BlockSpec((1, count, per), lambda i: (i, 0, 0)),
        out_shape=jax.ShapeDtypeStruct((chunks, count, per), half),
        scratch_shapes=[pltpu.VMEM((heads, width, width), single)],
        compiler_params=pltpu.CompilerParams(vmem_limit_bytes=VMEM),
        name="emit",
    )(place, everyone, starts, gain, *reads, *outs)


def mix_kernel(groups, *refs):
    rows, (w, out) = refs[:groups], refs[groups:]
    owners, _, width = rows[0].shape
    total = 0.0
    for owner in range(owners):
        for g in range(groups):
            first = (owner * groups + g) * width
            total += mm(rows[g][owner], w[first : first + width, :])
    out[...] = total.astype(half)


def mix(rows, w_whole):
    depth, columns = w_whole.shape
    count = rows[0].shape[1]
    tile = 512
    return pl.pallas_call(
        functools.partial(mix_kernel, len(rows)),
        grid=(columns // tile,),
        in_specs=[pl.BlockSpec(a.shape, lambda i: (0, 0, 0)) for a in rows]
        + [pl.BlockSpec((depth, tile), lambda i: (0, i))],
        out_specs=pl.BlockSpec((count, tile), lambda i: (0, i)),
        out_shape=jax.ShapeDtypeStruct((count, columns), half),
        compiler_params=pltpu.CompilerParams(vmem_limit_bytes=VMEM),
        name="mix",
    )(*rows, w_whole)


def whole_weight(w_out, seqs, owners):
    per, columns = w_out.shape
    place = lax.axis_index("seq")
    share = per // seqs
    mine = lax.dynamic_slice_in_dim(w_out, place * share, share, 0)
    turned = [mine]
    for shift in range(1, owners):
        pairs = [(i, (i + shift) % owners) for i in range(owners)]
        turned.append(lax.ppermute(mine, "head", pairs))
    turned = jnp.stack(turned)
    owner = lax.axis_index("head")
    held = jnp.stack(
        [
            lax.dynamic_index_in_dim(turned, (owner - i + owners) % owners, 0, False)
            for i in range(owners)
        ]
    )
    levels = seqs.bit_length() - 1
    turns = list(range(1, levels)) + [0]
    for bit in turns:
        pairs = [(i, i ^ (1 << bit)) for i in range(seqs)]
        other = lax.ppermute(held, "seq", pairs)
        upper = (place >> bit) & 1 == 1
        held = jnp.stack([jnp.where(upper, other, held), jnp.where(upper, held, other)])
    axes = [turns[::-1].index(bit) for bit in reversed(range(levels))]
    held = held.transpose([levels] + axes + [levels + 1, levels + 2])
    return held.reshape(owners * per, columns)


def body(seqs, owners, tokens, w_query, w_key, w_value, w_beta, beta_gain, norm_gain, w_out):
    per = w_query.shape[1]
    heads = w_beta.shape[1]
    place = lax.axis_index("seq")
    groups = 1
    few = heads // groups
    w_whole = whole_weight(w_out, seqs, owners)
    ends = [sum(CHUNKS[: i + 1]) for i in range(len(CHUNKS))]
    pieces = [
        lax.all_gather(tokens[end - size : end], "head", axis=0)
        for size, end in zip(CHUNKS, ends)
    ]
    weights = (w_query, w_key, w_value, w_beta, beta_gain)
    done = []
    for a in pieces:
        if done:
            a, done[-1] = lax.optimization_barrier((a, done[-1]))
        if len(done) == 1:
            a, w_whole = lax.optimization_barrier((a, w_whole))
        done.append([chunk_terms(a, *weights, few, g) for g in range(groups)])
    pairs = [fold([a[g][2] for a in done]) for g in range(groups)]
    everyone = [lax.all_gather(last, "seq", axis=0) for _, last in pairs]
    rows = []
    for g in range(groups):
        normed = emit(
            place.reshape(1).astype(jnp.int32),
            everyone[g],
            pairs[g][0],
            norm_gain[g * per // groups : (g + 1) * per // groups].reshape(1, -1),
            [a[g][0] for a in done],
            [a[g][1] for a in done],
        )
        rows.append(lax.all_to_all(normed, "head", split_axis=0, concat_axis=0, tiled=True))
    return mix(rows, w_whole)


def solution(mesh):
    placed = (
        P(("seq", "head"), None),
        P(None, "head"),
        P(None, "head"),
        P(None, "head"),
        P(None, "head"),
        P("head"),
        P("head"),
        P("head", None),
    )
    return jax.shard_map(
        functools.partial(body, mesh.shape["seq"], mesh.shape["head"]),
        mesh=mesh,
        in_specs=placed,
        out_specs=P(("seq", "head"), None),
        check_vma=False,
    )
```

```python
import functools

import jax
import jax.numpy as jnp
from jax import lax
from jax.experimental import pallas as pl
from jax.experimental.pallas import tpu as pltpu
from jax.sharding import PartitionSpec as P

LANES = 128
CHUNKS = (256, 256)
VMEM = 48 * 2**20
half = jnp.bfloat16
single = jnp.float32


def mm(left, right):
    return jnp.dot(left.astype(half), right.astype(half), preferred_element_type=single)


def mm_bt(left, right):
    return lax.dot_general(left, right, (((1,), (1,)), ((), ())), preferred_element_type=single)


def mm_t(left, right):
    return lax.dot_general(
        left, right.astype(half), (((0,), (0,)), ((), ())), preferred_element_type=single
    )


def unit(raw):
    return (raw * lax.rsqrt(jnp.sum(raw * raw, -1, keepdims=True) + 1e-06)).astype(half)


def chunk_kernel(heads, tok, wq, wk, wv, wb, gain, reads_ref, outs_ref, trans_ref):
    width = wq.shape[1] // heads
    x = tok[0]
    size = x.shape[0]
    each = range(heads)

    def project(w):
        full = jnp.dot(x, w[...], preferred_element_type=single).astype(half).astype(single)
        return [full[:, h * width : (h + 1) * width] for h in each]

    k = [unit(a) for a in project(wk)]
    beta = gain[...] * jax.nn.sigmoid(jnp.dot(x, wb[...], preferred_element_type=single))
    rates = [beta[:, h : h + 1] for h in each]
    row = lax.broadcasted_iota(jnp.int32, (size, size), 0)
    col = lax.broadcasted_iota(jnp.int32, (size, size), 1)
    near = (row // 16) == (col // 16)
    mid = (row // 64) == (col // 64)
    below = row > col
    eye = jnp.where(row == col, 1.0, 0.0).astype(single)
    lower = [jnp.where(below, rates[h] * mm_bt(k[h], k[h]), 0.0) for h in each]
    power = [jnp.where(near, a, 0.0) for a in lower]
    inverse = [eye - a for a in power]
    for level in range(3):
        power = [mm(a, a) for a in power]
        inverse = [t + mm(t, a) for t, a in zip(inverse, power)]
    rest = [mm(t, jnp.where(mid & ~near, a, 0.0)) for t, a in zip(inverse, lower)]
    inverse = [t - mm(r, t) for r, t in zip(rest, inverse)]
    rest = [mm(r, r) for r in rest]
    inverse = [t + mm(r, t) for r, t in zip(rest, inverse)]
    rest = [mm(t, jnp.where(mid, 0.0, a)) for t, a in zip(inverse, lower)]
    v = project(wv)
    terms = [jnp.concatenate([rates[h] * k[h].astype(single), rates[h] * v[h]], 1) for h in each]
    terms = [mm(t, a) for t, a in zip(inverse, terms)]
    terms = [t - mm(r, t) for r, t in zip(rest, terms)]
    rest = [mm(r, r) for r in rest]
    terms = [(t + mm(r, t)).astype(half) for r, t in zip(rest, terms)]
    q = [unit(a) for a in project(wq)]
    for h in each:
        causal = jnp.where(below | (row == col), mm_bt(q[h], k[h]), 0.0)
        read = mm(causal, terms[h])
        here = slice(h * width, (h + 1) * width)
        reads_ref[0, :, here] = (q[h].astype(single) - read[:, :width]).astype(half)
        outs_ref[0, :, here] = read[:, width:]
        trans_ref[0, h] = mm_t(k[h], terms[h])


def chunk_terms(tokens, wq, wk, wv, wb, gain, heads, group):
    chunks, size, depth = tokens.shape
    width = wq.shape[1] // wb.shape[1]
    per = heads * width
    gain = jnp.pad(gain[group * heads : (group + 1) * heads], (0, LANES - heads))
    gain = gain.reshape(1, LANES)
    wb = wb[:, group * heads : (group + 1) * heads]
    wb = jnp.pad(wb, ((0, 0), (0, LANES - heads)))

    def once(shape):
        return pl.BlockSpec(shape, lambda i: (0,) * len(shape), pipeline_mode=pl.Buffered(1))

    return pl.pallas_call(
        functools.partial(chunk_kernel, heads),
        grid=(chunks,),
        in_specs=[pl.BlockSpec((1, size, depth), lambda i: (i, 0, 0))]
        + [
            pl.BlockSpec((depth, per), lambda i: (0, group), pipeline_mode=pl.Buffered(1))
            for _ in range(3)
        ]
        + [once(w.shape) for w in (wb, gain)],
        out_specs=[
            pl.BlockSpec((1, size, per), lambda i: (i, 0, 0)),
            pl.BlockSpec((1, size, per), lambda i: (i, 0, 0)),
            pl.BlockSpec((1, heads, width, 2 * width), lambda i: (i, 0, 0, 0)),
        ],
        out_shape=[
            jax.ShapeDtypeStruct((chunks, size, per), half),
            jax.ShapeDtypeStruct((chunks, size, per), single),
            jax.ShapeDtypeStruct((chunks, heads, width, 2 * width), single),
        ],
        compiler_params=pltpu.CompilerParams(vmem_limit_bytes=VMEM),
        cost_estimate=pl.CostEstimate(
            flops=2 * chunks * size * (depth * 3 * per + heads * 18 * size * size),
            bytes_accessed=2 * depth * 3 * per + chunks * size * (2 * depth + 8 * per),
            transcendentals=0,
        ),
        name="chunk_terms",
    )(tokens, wq, wk, wv, wb, gain)


def fold_kernel(parts, *refs):
    trans, (starts_ref, last_ref) = refs[:parts], refs[parts:]
    chunks, heads, width, _ = trans[0].shape
    row = lax.broadcasted_iota(jnp.int32, (width, 2 * width), 0)
    col = lax.broadcasted_iota(jnp.int32, (width, 2 * width), 1)
    state = [jnp.where(row == col, 1.0, 0.0).astype(single) for _ in range(heads)]
    for place in range(chunks):
        for part in range(parts):
            for h in range(heads):
                starts_ref[part, place, h] = state[h]
                step = trans[part][place, h]
                moved = state[h] - mm(step[:, :width], state[h])
                state[h] = moved + jnp.where(col < width, 0.0, step)
    for h in range(heads):
        last_ref[h] = state[h].astype(half)


def fold(trans):
    chunks, heads, width, wide = trans[0].shape
    parts = len(trans)
    return pl.pallas_call(
        functools.partial(fold_kernel, parts),
        out_shape=[
            jax.ShapeDtypeStruct((parts, chunks, heads, width, wide), single),
            jax.ShapeDtypeStruct((heads, width, wide), half),
        ],
        compiler_params=pltpu.CompilerParams(vmem_limit_bytes=VMEM),
        name="fold",
    )(*trans)


def emit_kernel(parts, place_ref, all_ref, starts_ref, gain, *refs):
    reads, outs, (result, entry) = refs[:parts], refs[parts : 2 * parts], refs[2 * parts :]
    heads, width, _ = entry.shape

    @pl.when(pl.program_id(0) == 0)
    def _():
        entry[...] = jnp.zeros_like(entry)

        def one(turn, carry):
            for h in range(heads):
                pair = all_ref[turn, h]
                entry[h] = mm(pair[:, :width], entry[h]) + pair[:, width:].astype(single)
            return carry

        lax.fori_loop(0, place_ref[0], one, 0)

    first = 0
    for part in range(parts):
        rows = slice(first, first + reads[part].shape[1])
        first = rows.stop
        for h in range(heads):
            here = slice(h * width, (h + 1) * width)
            pair = starts_ref[0, 0, h]
            state = mm(pair[:, :width], entry[h]) + pair[:, width:]
            o = mm(reads[part][0, :, here], state) + outs[part][0, :, here]
            scale = lax.rsqrt(jnp.mean(o * o, -1, keepdims=True) + 1e-05)
            result[0, rows, here] = (o * scale * gain[:, here]).astype(half)


def emit(part, place, everyone, starts, gain, reads, outs):
    parts = len(reads)
    chunks, _, per = reads[0].shape
    _, _, heads, width, wide = starts.shape
    rows = [pl.BlockSpec((1, a.shape[1], per), lambda i: (i, 0, 0)) for a in reads]
    count = sum(a.shape[1] for a in reads)
    return pl.pallas_call(
        functools.partial(emit_kernel, parts),
        grid=(chunks,),
        in_specs=[
            pl.BlockSpec(memory_space=pltpu.SMEM),
            pl.BlockSpec(
                everyone.shape, lambda i: (0, 0, 0, 0), pipeline_mode=pl.Buffered(1)
            ),
            pl.BlockSpec((1, 1, heads, width, wide), lambda i: (part, i, 0, 0, 0)),
            pl.BlockSpec((1, per), lambda i: (0, 0)),
        ]
        + rows * 2,
        out_specs=pl.BlockSpec((1, count, per), lambda i: (i, 0, 0)),
        out_shape=jax.ShapeDtypeStruct((chunks, count, per), half),
        scratch_shapes=[pltpu.VMEM((heads, width, width), single)],
        compiler_params=pltpu.CompilerParams(vmem_limit_bytes=VMEM),
        name="emit",
    )(place, everyone, starts, gain, *reads, *outs)


def mix_kernel(parts, *refs):
    rows, (w, out) = refs[:parts], refs[parts:]
    first = 0
    for part in rows:
        owners, count, width = part.shape
        total = mm(part[0], w[:width, :])
        for owner in range(1, owners):
            total += mm(part[owner], w[owner * width : (owner + 1) * width, :])
        out[first : first + count, :] = total.astype(half)
        first += count


def mix(rows, w_whole):
    depth, columns = w_whole.shape
    count = sum(a.shape[1] for a in rows)
    tile = 512
    return pl.pallas_call(
        functools.partial(mix_kernel, len(rows)),
        grid=(columns // tile,),
        in_specs=[pl.BlockSpec(a.shape, lambda i: (0, 0, 0)) for a in rows]
        + [pl.BlockSpec((depth, tile), lambda i: (0, i))],
        out_specs=pl.BlockSpec((count, tile), lambda i: (0, i)),
        out_shape=jax.ShapeDtypeStruct((count, columns), half),
        compiler_params=pltpu.CompilerParams(vmem_limit_bytes=VMEM),
        name="mix",
    )(*rows, w_whole)


def whole_weight(w_out, seqs, owners):
    per, columns = w_out.shape
    place = lax.axis_index("seq")
    share = per // seqs
    mine = lax.dynamic_slice_in_dim(w_out, place * share, share, 0)
    turned = [mine]
    for shift in range(1, owners):
        pairs = [(i, (i + shift) % owners) for i in range(owners)]
        turned.append(lax.ppermute(mine, "head", pairs))
    turned = jnp.stack(turned)
    owner = lax.axis_index("head")
    held = jnp.stack(
        [
            lax.dynamic_index_in_dim(turned, (owner - i + owners) % owners, 0, False)
            for i in range(owners)
        ]
    )
    levels = seqs.bit_length() - 1
    turns = list(range(1, levels)) + [0]
    for bit in turns:
        pairs = [(i, i ^ (1 << bit)) for i in range(seqs)]
        other = lax.ppermute(held, "seq", pairs)
        upper = (place >> bit) & 1 == 1
        held = jnp.stack([jnp.where(upper, other, held), jnp.where(upper, held, other)])
    axes = [turns[::-1].index(bit) for bit in reversed(range(levels))]
    held = held.transpose([levels] + axes + [levels + 1, levels + 2])
    return held.reshape(owners * per, columns)


def body(seqs, owners, tokens, w_query, w_key, w_value, w_beta, beta_gain, norm_gain, w_out):
    per = w_query.shape[1]
    heads = w_beta.shape[1]
    place = lax.axis_index("seq")
    w_whole = whole_weight(w_out, seqs, owners)
    ends = [sum(CHUNKS[: i + 1]) for i in range(len(CHUNKS))]
    pieces = [
        lax.all_gather(tokens[end - size : end], "head", axis=0)
        for size, end in zip(CHUNKS, ends)
    ]
    weights = (w_query, w_key, w_value, w_beta, beta_gain)
    done = []
    for a in pieces:
        if len(done) == 1:
            a, done[-1], w_whole = lax.optimization_barrier((a, done[-1], w_whole))
        done.append(chunk_terms(a, *weights, heads, 0))
    starts, last = fold([a[2] for a in done])
    everyone = lax.all_gather(last, "seq", axis=0)
    where = place.reshape(1).astype(jnp.int32)
    gain = norm_gain.reshape(1, per)
    rows = []
    for part, (reads, outs, _) in enumerate(done):
        normed = emit(part, where, everyone, starts, gain, [reads], [outs])
        rows.append(lax.all_to_all(normed, "head", split_axis=0, concat_axis=0, tiled=True))
    return mix(rows, w_whole)


def solution(mesh):
    placed = (
        P(("seq", "head"), None),
        P(None, "head"),
        P(None, "head"),
        P(None, "head"),
        P(None, "head"),
        P("head"),
        P("head"),
        P("head", None),
    )
    return jax.shard_map(
        functools.partial(body, mesh.shape["seq"], mesh.shape["head"]),
        mesh=mesh,
        in_specs=placed,
        out_specs=P(("seq", "head"), None),
        check_vma=False,
    )
```
